256 devices in a mesh: occ: 32 (over z, x_lo, core), aux: 8 (over x_hi, y).
Axes of the slice: x: 4 (x_hi: 2, x_lo: 2; x = x_hi * 2 + x_lo), y: 4, z: 8, core: 2. Of those that a mesh axis runs over, the one named last changes fastest.
Arguments:
- b_factor: bfloat16 [1024, 16, 49152], P('occ', None, 'aux'), may hold values from -0.40234375 to 0.40234375
- occ_energy: float32 [1024], P('occ'), may hold values from -3 to -0.5
- virt_energy: float32 [16], replicated, may hold values from 0.2 to 4
Outputs:
- gamma: bfloat16 [1024, 16, 49152], P('occ', None, 'aux')
The draws below stay inside these ranges and needn't reach their ends.
All inputs are finite; a program needn't handle non-finite values.
Results may differ from the reference program's by a relative error of at most 0.022.
Values may be sent and summed in bfloat16 or wider, within the bound.
No kernel may reach another device: no remote copies, remote signals or barrier semaphores. Data moves between devices by JAX's collectives and lax.ppermute only.
A program may use at most 128 MiB of HBM per device.

```python
import jax
import jax.numpy as jnp
from jax import lax

OCC = 1024
AUX = 49152
SLAB = 16
OCC_DEV = 32
N_OCC = 32


def block_scale(rng, shape, split, smallest, largest):
    gain = 1.0
    for dim, parts in split:
        steps = jax.random.uniform(jax.random.fold_in(jax.random.fold_in(rng, 6), dim), (parts,), jnp.float32, smallest / len(split), largest / len(split))
        gain = gain * jnp.repeat(jnp.exp(steps), shape[dim] // parts).reshape((-1,) + (1,) * (len(shape) - 1 - dim))
    return gain


def normal_values(rng, shape, width, bound, pieces=(), kind=jnp.bfloat16):
    array = width * jax.random.normal(rng, shape, jnp.float32)
    if pieces:
        array = array * block_scale(rng, shape, pieces, -0.22, 0.18)
    return jnp.clip(array, -bound, bound).astype(kind)


def setup_inputs(seed: int = 0) -> dict:
    key_of = jax.random.split(jax.random.key(seed), 4)
    b_factor = normal_values(key_of[0], (OCC, SLAB, AUX), (AUX ** -0.25), 0.40234375, ((0, 32), (2, 8)))
    occ_energy = jnp.clip(-3.0 + 2.5 * jax.random.uniform(key_of[1], (OCC,), jnp.float32) ** block_scale(key_of[1], (OCC,), ((0, 32),), -0.2, 0.2), -3.0, -0.5)
    virt_energy = jnp.clip(jax.random.uniform(key_of[2], (SLAB,), jnp.float32, 0.2, 4.0), 0.2, 4.0)
    return dict(b_factor=b_factor, occ_energy=occ_energy, virt_energy=virt_energy)


def block_gamma(b_factor, occ_energy, virt_energy, block):
    own_rows = lax.dynamic_slice_in_dim(b_factor, (block * OCC_DEV).astype(jnp.int32), OCC_DEV, 0).reshape(OCC_DEV * SLAB, AUX)
    own_energy = lax.dynamic_slice_in_dim(occ_energy, (block * OCC_DEV).astype(jnp.int32), OCC_DEV, 0)
    gamma_sum = jnp.zeros((OCC_DEV * SLAB, AUX), jnp.float32)
    for offset in (1, 2):
        partner = ((block - offset) % N_OCC).astype(jnp.int32)
        partner_rows = lax.dynamic_slice_in_dim(b_factor, (partner * OCC_DEV).astype(jnp.int32), OCC_DEV, 0).reshape(OCC_DEV * SLAB, AUX)
        partner_energy = lax.dynamic_slice_in_dim(occ_energy, (partner * OCC_DEV).astype(jnp.int32), OCC_DEV, 0)
        integrals = jnp.dot(own_rows, partner_rows.T, preferred_element_type=jnp.float32).reshape(OCC_DEV, SLAB, OCC_DEV, SLAB)
        denominator = (own_energy[:, None, None, None] + partner_energy[None, None, :, None]
                       - virt_energy[None, :, None, None] - virt_energy[None, None, None, :])
        amplitude = ((2.0 * integrals - integrals.transpose(0, 3, 2, 1)) / denominator).astype(jnp.bfloat16)
        gamma_sum = gamma_sum + jnp.dot(amplitude.reshape(OCC_DEV * SLAB, OCC_DEV * SLAB), partner_rows, preferred_element_type=jnp.float32)
    return gamma_sum.astype(jnp.bfloat16).reshape(OCC_DEV, SLAB, AUX)


def reference(b_factor, occ_energy, virt_energy):
    blocks = jnp.arange(N_OCC, dtype=jnp.int32)
    result = lax.map(lambda block: block_gamma(b_factor, occ_energy, virt_energy, block), blocks)
    return result.reshape(OCC, SLAB, AUX)
```

```python
import functools

import jax
import jax.numpy as jnp
from jax import lax
from jax.experimental import pallas as pl
from jax.experimental.pallas import tpu as pltpu
from jax.sharding import PartitionSpec as P

VMEM_BYTES = 40 * 1024 * 1024


def after(value, *earlier):
    return lax.optimization_barrier((value,) + earlier)[0]


def stacked(refs):
    blocks = [ref[...] for ref in refs]
    return blocks[0] if len(blocks) == 1 else jnp.concatenate(blocks, axis=0)


def product_kernel(n_left, n_right, at_ref, *refs):
    left, right = refs[:n_left], refs[n_left:n_left + n_right]
    out_ref, total = refs[n_left + n_right:]
    step = pl.program_id(0)
    term = lax.dot_general(
        stacked(left), stacked(right), (((1,), (1,)), ((), ())), preferred_element_type=jnp.float32
    )

    @pl.when(step == 0)
    def _():
        total[...] = term

    @pl.when(step > 0)
    def _():
        total[...] += term

    @pl.when(step == pl.num_programs(0) - 1)
    def _():
        out_ref[...] = total[...].astype(out_ref.dtype)


def products(left, right, left_at, right_at, depth, tile):
    rows = sum(array.shape[0] for array in left)
    cols = sum(array.shape[0] for array in right)
    offsets = jnp.stack([jnp.asarray(left_at, jnp.int32), jnp.asarray(right_at, jnp.int32)])
    return pl.pallas_call(
        functools.partial(product_kernel, len(left), len(right)),
        out_shape=jax.ShapeDtypeStruct((rows, cols), jnp.bfloat16),
        grid_spec=pltpu.PrefetchScalarGridSpec(
            num_scalar_prefetch=1,
            grid=(depth // tile,),
            in_specs=[pl.BlockSpec((a.shape[0], tile), lambda c, at: (0, at[0] + c)) for a in left]
            + [pl.BlockSpec((a.shape[0], tile), lambda c, at: (0, at[1] + c)) for a in right],
            out_specs=pl.BlockSpec((rows, cols), lambda c, at: (0, 0)),
            scratch_shapes=[pltpu.VMEM((rows, cols), jnp.float32)],
        ),
        compiler_params=pltpu.CompilerParams(vmem_limit_bytes=VMEM_BYTES),
        cost_estimate=pl.CostEstimate(
            flops=2 * rows * cols * depth, bytes_accessed=2 * (rows + cols) * depth, transcendentals=0
        ),
        name="products",
    )(offsets, *left, *right)


def swapped(x, width):
    rows, cols = x.shape
    r = lax.broadcasted_iota(jnp.int32, x.shape, 0)
    c = lax.broadcasted_iota(jnp.int32, x.shape, 1)
    s = 1
    while s < width:
        below = pltpu.roll(pltpu.roll(x, rows - s, 0), s, 1)
        above = pltpu.roll(pltpu.roll(x, s, 0), cols - s, 1)
        r_bit, c_bit = (r & s) != 0, (c & s) != 0
        x = jnp.where(r_bit == c_bit, x, jnp.where(c_bit, below, above))
        s *= 2
    return x


def amplitude_kernel(width, parts_ref, other_ref, row_ref, col_ref, out_ref):
    x = other_ref[...]
    for part in range(parts_ref.shape[0]):
        x = x + parts_ref[part].astype(jnp.float32)
    out_ref[...] = ((2.0 * x - swapped(x, width)) / (row_ref[...] + col_ref[...])).astype(out_ref.dtype)


def amplitudes(parts, other, row, col, width):
    return pl.pallas_call(
        functools.partial(amplitude_kernel, width),
        out_shape=jax.ShapeDtypeStruct(other.shape, jnp.bfloat16),
        compiler_params=pltpu.CompilerParams(vmem_limit_bytes=VMEM_BYTES),
        cost_estimate=pl.CostEstimate(flops=60 * other.size, bytes_accessed=2 * parts.size, transcendentals=0),
        name="amplitudes",
    )(parts, other, row, col)


def density_kernel(n_late, at_ref, amp_early, amp_late, early, *refs):
    late, out_ref = refs[:n_late], refs[-1]
    total = jnp.dot(amp_early[...], early[...], preferred_element_type=jnp.float32)
    total = total + jnp.dot(amp_late[...], stacked(late), preferred_element_type=jnp.float32)
    out_ref[...] = total.astype(out_ref.dtype)


def density(out, amp_early, amp_late, early, late, at, tile):
    rows, width = early.shape
    cols = late[0].shape[1]
    in_specs = [
        pl.BlockSpec(amp_early.shape, lambda c, at: (0, 0)),
        pl.BlockSpec(amp_late.shape, lambda c, at: (0, 0)),
        pl.BlockSpec((rows, tile), lambda c, at: (0, c)),
    ] + [pl.BlockSpec((a.shape[0], tile), lambda c, at: (0, at[0] + c)) for a in late]
    operands = [jnp.reshape(at, (1,)).astype(jnp.int32), amp_early, amp_late, early, *late]
    aliases = {}
    if out is not None:
        in_specs.append(pl.BlockSpec(memory_space=pl.ANY))
        aliases = {len(operands): 0}
        operands.append(out)
    return pl.pallas_call(
        functools.partial(density_kernel, len(late)),
        out_shape=jax.ShapeDtypeStruct((amp_early.shape[0], cols), jnp.bfloat16),
        grid_spec=pltpu.PrefetchScalarGridSpec(
            num_scalar_prefetch=1,
            grid=(width // tile,),
            in_specs=in_specs,
            out_specs=pl.BlockSpec((amp_early.shape[0], tile), lambda c, at: (0, at[0] + c)),
        ),
        input_output_aliases=aliases,
        compiler_params=pltpu.CompilerParams(vmem_limit_bytes=VMEM_BYTES),
        cost_estimate=pl.CostEstimate(
            flops=4 * rows * rows * width, bytes_accessed=6 * rows * width, transcendentals=0
        ),
        name="density",
    )(*operands)


def per_device(b_factor, occ_energy, virt_energy):
    occ_rows, slab, cols = b_factor.shape
    rows, half = occ_rows * slab, cols // 2
    n_occ, n_aux = lax.axis_size("occ"), lax.axis_size("aux")
    p, q = lax.axis_index("occ"), lax.axis_index("aux")
    core, parity = p % 2, (p // 2) % 2
    own_rows = rows // n_aux
    depth_tile, out_tile = cols // 6, cols // 24
    n_o, n_e = 4, 2

    ring = [(i, (i + 1) % n_occ) for i in range(n_occ)]
    in_chip = [(i, i + 1) for i in range(0, n_occ, 2)]
    to_next_chip = [(i, (i + 1) % n_occ) for i in range(1, n_occ, 2)]
    chip_before_last = [(i, (i - 4) % n_occ) for i in range(0, n_occ, 2)]
    evens_to_next = [(i, (i + 2) % n_occ) for i in range(0, n_occ, 2)]

    def send(value, pairs):
        return lax.ppermute(value, "occ", pairs)

    own = b_factor.reshape(rows, cols)
    energy_near = send(occ_energy, ring)
    energy_far = send(occ_energy, [(i, (i + 2) % n_occ) for i in range(n_occ)])

    even = send(own, in_chip)
    first = core == 0
    even_source = jnp.where(first, own, even)
    early_half = (parity + core + 1) % 2
    o_rows, e_rows = rows // n_o, rows // n_e

    def odd_part(part, *earlier):
        return send(after(own[part * o_rows:(part + 1) * o_rows], *earlier), to_next_chip)

    def early_part(part, *earlier):
        block = lax.dynamic_slice(even_source, (part * e_rows, parity * half), (e_rows, half))
        return send(after(block, *earlier), ring)

    def last_part(start, size, *earlier):
        block = lax.dynamic_slice(even_source, (0, (1 - parity) * half + start), (rows, size))
        return send(after(block, *earlier), ring)

    odd = [odd_part(0)]
    early = [early_part(0), early_part(1, odd[0])]
    odd.append(odd_part(1, early[0]))
    odd.append(odd_part(2, early[1]))
    odd.append(odd_part(3, odd[1]))
    sizes = (half // 2, half // 4, half // 4)
    last = [last_part(0, sizes[0], odd[2])]
    last.append(last_part(sizes[0], sizes[1], odd[3]))
    last.append(last_part(sizes[0] + sizes[1], sizes[2], last[0]))

    back = [send(part, chip_before_last) for part in early]
    partner = [jnp.where(first, part, send(part, in_chip)) for part in odd]

    half_tiles = half // depth_tile
    near_half = products([own], early, early_half * half_tiles, 0, half, depth_tile)
    far_half = lax.cond(
        first,
        lambda: products(back, [own], 0, early_half * half_tiles, half, depth_tile),
        lambda: products(
            [own], [even], (1 - early_half) * half_tiles, (1 - early_half) * half_tiles, half, depth_tile
        ),
    )

    def spread(value):
        return lax.all_to_all(value.reshape(n_aux, own_rows, rows), "aux", 0, 0)

    near_parts = spread(near_half)
    far_sum = spread(far_half).astype(jnp.float32).sum(0)
    other = jnp.where(first, send(far_sum, evens_to_next), far_sum)

    row = (occ_energy[:, None] - virt_energy[None, :]).reshape(rows, 1)
    row = lax.dynamic_slice(row, (q * own_rows, 0), (own_rows, 1))

    def partner_energy(near):
        energy = jnp.where(near, energy_near, energy_far)
        return (energy[:, None] - virt_energy[None, :]).reshape(1, rows)

    amp_even = amplitudes(near_parts, other, row, partner_energy(core == 1), slab)
    amp_even = lax.all_gather(amp_even, "aux", axis=0, tiled=True)

    odd_products = jnp.concatenate(
        [products([own], partner[:2], 0, 0, cols, depth_tile), products([own], partner[2:], 0, 0, cols, depth_tile)],
        axis=1,
    )
    amp_odd = amplitudes(
        spread(odd_products), jnp.zeros((own_rows, rows), jnp.float32), row, partner_energy(first), slab
    )
    amp_odd = lax.all_gather(amp_odd, "aux", axis=0, tiled=True)

    tiles = half // out_tile
    early_block = jnp.concatenate(early, axis=0)
    gamma = density(None, amp_even, amp_odd, early_block, partner, early_half * tiles, out_tile)
    start = 0
    for block, size in zip(last, sizes):
        at = (1 - early_half) * tiles + start // out_tile
        gamma = density(gamma, amp_even, amp_odd, block, partner, at, out_tile)
        start += size
    return gamma.reshape(occ_rows, slab, cols)


def solution(mesh):
    placed = (P("occ", None, "aux"), P("occ"), P())
    return jax.shard_map(
        per_device, mesh=mesh, in_specs=placed, out_specs=P("occ", None, "aux"), check_vma=False
    )
```

```python
import functools

import jax
import jax.numpy as jnp
from jax import lax
from jax.experimental import pallas as pl
from jax.experimental.pallas import tpu as pltpu
from jax.sharding import PartitionSpec as P

VMEM_BYTES = 40 * 1024 * 1024


def after(value, *earlier):
    return lax.optimization_barrier((value,) + earlier)[0]


def stacked(refs):
    blocks = [ref[...] for ref in refs]
    return blocks[0] if len(blocks) == 1 else jnp.concatenate(blocks, axis=0)


def product_kernel(n_left, n_right, at_ref, *refs):
    left, right = refs[:n_left], refs[n_left:n_left + n_right]
    out_ref, total = refs[n_left + n_right:]
    step = pl.program_id(0)
    term = lax.dot_general(
        stacked(left), stacked(right), (((1,), (1,)), ((), ())), preferred_element_type=jnp.float32
    )

    @pl.when(step == 0)
    def _():
        total[...] = term

    @pl.when(step > 0)
    def _():
        total[...] += term

    @pl.when(step == pl.num_programs(0) - 1)
    def _():
        out_ref[...] = total[...].astype(out_ref.dtype)


def products(left, right, left_at, right_at, depth, tile):
    rows = sum(array.shape[0] for array in left)
    cols = sum(array.shape[0] for array in right)
    offsets = jnp.stack([jnp.asarray(left_at, jnp.int32), jnp.asarray(right_at, jnp.int32)])
    return pl.pallas_call(
        functools.partial(product_kernel, len(left), len(right)),
        out_shape=jax.ShapeDtypeStruct((rows, cols), jnp.bfloat16),
        grid_spec=pltpu.PrefetchScalarGridSpec(
            num_scalar_prefetch=1,
            grid=(depth // tile,),
            in_specs=[pl.BlockSpec((a.shape[0], tile), lambda c, at: (0, at[0] + c)) for a in left]
            + [pl.BlockSpec((a.shape[0], tile), lambda c, at: (0, at[1] + c)) for a in right],
            out_specs=pl.BlockSpec((rows, cols), lambda c, at: (0, 0)),
            scratch_shapes=[pltpu.VMEM((rows, cols), jnp.float32)],
        ),
        compiler_params=pltpu.CompilerParams(vmem_limit_bytes=VMEM_BYTES),
        cost_estimate=pl.CostEstimate(
            flops=2 * rows * cols * depth, bytes_accessed=2 * (rows + cols) * depth, transcendentals=0
        ),
        name="products",
    )(offsets, *left, *right)


def swapped(x, width):
    rows, cols = x.shape
    r = lax.broadcasted_iota(jnp.int32, x.shape, 0)
    c = lax.broadcasted_iota(jnp.int32, x.shape, 1)
    s = 1
    while s < width:
        below = pltpu.roll(pltpu.roll(x, rows - s, 0), s, 1)
        above = pltpu.roll(pltpu.roll(x, s, 0), cols - s, 1)
        r_bit, c_bit = (r & s) != 0, (c & s) != 0
        x = jnp.where(r_bit == c_bit, x, jnp.where(c_bit, below, above))
        s *= 2
    return x


def amplitude_kernel(width, sum_ref, other_ref, row_ref, col_ref, out_ref):
    x = sum_ref[...] + other_ref[...].astype(jnp.float32)
    out_ref[...] = ((2.0 * x - swapped(x, width)) / (row_ref[...] + col_ref[...])).astype(out_ref.dtype)


def amplitudes(partial_sum, other, row, col, width):
    return pl.pallas_call(
        functools.partial(amplitude_kernel, width),
        out_shape=jax.ShapeDtypeStruct(other.shape, jnp.bfloat16),
        compiler_params=pltpu.CompilerParams(vmem_limit_bytes=VMEM_BYTES),
        cost_estimate=pl.CostEstimate(flops=60 * other.size, bytes_accessed=8 * other.size, transcendentals=0),
        name="amplitudes",
    )(partial_sum, other, row, col)


def density_kernel(n_early, n_late, at_ref, amp_early, amp_late, *refs):
    early, late, out_ref = refs[:n_early], refs[n_early:n_early + n_late], refs[-1]
    total = jnp.dot(amp_early[...], stacked(early), preferred_element_type=jnp.float32)
    total = total + jnp.dot(amp_late[...], stacked(late), preferred_element_type=jnp.float32)
    out_ref[...] = total.astype(out_ref.dtype)


def density(out, amp_early, amp_late, early, late, at, tile):
    rows, width, cols = amp_early.shape[0], early[0].shape[1], late[0].shape[1]
    in_specs = (
        [pl.BlockSpec(amp_early.shape, lambda c, at: (0, 0)), pl.BlockSpec(amp_late.shape, lambda c, at: (0, 0))]
        + [pl.BlockSpec((a.shape[0], tile), lambda c, at: (0, c)) for a in early]
        + [pl.BlockSpec((a.shape[0], tile), lambda c, at: (0, at[0] + c)) for a in late]
    )
    operands = [jnp.reshape(at, (1,)).astype(jnp.int32), amp_early, amp_late, *early, *late]
    aliases = {}
    if out is not None:
        in_specs.append(pl.BlockSpec(memory_space=pl.ANY))
        aliases = {len(operands): 0}
        operands.append(out)
    return pl.pallas_call(
        functools.partial(density_kernel, len(early), len(late)),
        out_shape=jax.ShapeDtypeStruct((rows, cols), jnp.bfloat16),
        grid_spec=pltpu.PrefetchScalarGridSpec(
            num_scalar_prefetch=1,
            grid=(width // tile,),
            in_specs=in_specs,
            out_specs=pl.BlockSpec((rows, tile), lambda c, at: (0, at[0] + c)),
        ),
        input_output_aliases=aliases,
        compiler_params=pltpu.CompilerParams(vmem_limit_bytes=VMEM_BYTES),
        cost_estimate=pl.CostEstimate(
            flops=4 * rows * rows * width, bytes_accessed=6 * rows * width, transcendentals=0
        ),
        name="density",
    )(*operands)


def per_device(b_factor, occ_energy, virt_energy):
    occ_rows, slab, cols = b_factor.shape
    rows, half = occ_rows * slab, cols // 2
    n_occ, n_aux = lax.axis_size("occ"), lax.axis_size("aux")
    p, q = lax.axis_index("occ"), lax.axis_index("aux")
    core, parity = p % 2, (p // 2) % 2
    first = core == 0
    n_y = n_aux // 2
    y_groups = [list(range(n_y)), list(range(n_y, n_aux))]
    own_rows = rows // n_y
    depth_tile, wide_tile, tile = cols // 6, cols // 8, cols // 16

    ring = [(i, (i + 1) % n_occ) for i in range(n_occ)]
    two_on = [(i, (i + 2) % n_occ) for i in range(n_occ)]
    in_chip = [(i, i + 1) for i in range(0, n_occ, 2)]
    to_next_chip = [(i, (i + 1) % n_occ) for i in range(1, n_occ, 2)]
    two_chips_back = [(i, (i - 4) % n_occ) for i in range(0, n_occ, 2)]
    evens_to_next = [(i, (i + 2) % n_occ) for i in range(0, n_occ, 2)]
    other_x = [(i, (i + n_y) % n_aux) for i in range(n_aux)]

    def send(value, pairs):
        return lax.ppermute(value, "occ", pairs)

    own = b_factor.reshape(rows, cols)
    energy_near, energy_far = send(occ_energy, ring), send(occ_energy, two_on)
    ready_own = after(own, energy_near, energy_far)

    o_starts = [0, 3 * rows // 16, 3 * rows // 4]
    o_sizes = [3 * rows // 16, 9 * rows // 16, rows // 4]
    odd = [send(ready_own[:o_sizes[0]], to_next_chip)]
    even = send(ready_own, in_chip)
    later_own = after(own, even)
    early_half = (parity + core + 1) % 2
    l_cols = half // 4

    def odd_part(part, *earlier):
        start = o_starts[part]
        return send(after(later_own[start:start + o_sizes[part]], *earlier), to_next_chip)

    def even_block(start, size):
        return jnp.where(
            first, lax.dynamic_slice(later_own, start, size), lax.dynamic_slice(even, start, size)
        )

    last_blocks = [even_block((0, (1 - parity) * half + part * l_cols), (rows, l_cols)) for part in range(4)]

    def last_part(part, *earlier):
        return send(after(last_blocks[part], *earlier), ring)

    def partner_part(part):
        return jnp.where(first, part, send(part, in_chip))

    partner = [partner_part(odd[0])]
    e_rows = rows // 2
    early = [send(after(even_block((0, parity * half), (e_rows, half)), odd[0]), ring)]
    early.append(send(after(even_block((e_rows, parity * half), (e_rows, half)), early[0]), ring))
    back = [send(part, two_chips_back) for part in early]
    odd.append(odd_part(1, early[1]))
    def spread_sum(value):
        parts = lax.all_to_all(value.reshape(n_y, own_rows, rows), "aux", 0, 0, axis_index_groups=y_groups)
        return parts.astype(jnp.float32).sum(0)

    def collected(value):
        parts = jnp.broadcast_to(value, (n_y, own_rows, rows))
        return lax.all_to_all(parts, "aux", 0, 0, axis_index_groups=y_groups).reshape(rows, rows)

    def slab_amplitudes(partial_sum, energy):
        other = lax.ppermute(partial_sum.astype(jnp.bfloat16), "aux", other_x)
        col = (energy[:, None] - virt_energy[None, :]).reshape(1, rows)
        return amplitudes(partial_sum, other, row, col, slab)

    row = (occ_energy[:, None] - virt_energy[None, :]).reshape(rows, 1)
    row = lax.dynamic_slice(row, ((q % n_y) * own_rows, 0), (own_rows, 1))
    even_energy = jnp.where(first, energy_far, energy_near)
    odd_energy = jnp.where(first, energy_near, energy_far)

    half_tiles = half // depth_tile
    near_half = products([own], [after(part, *last_blocks) for part in early], early_half * half_tiles, 0, half, depth_tile)
    near_sum = spread_sum(near_half)
    back = [after(part, near_sum) for part in back]
    far_half = lax.cond(
        first,
        lambda: products(back, [own], 0, early_half * half_tiles, half, depth_tile),
        lambda: products(
            [own], [even], (1 - early_half) * half_tiles, (1 - early_half) * half_tiles, half, depth_tile
        ),
    )
    odd.append(odd_part(2, odd[1], far_half))
    last = [last_part(0, odd[2])]
    last.append(last_part(1, odd[2]))
    far_sum = spread_sum(far_half)
    far_sum = jnp.where(
        first, send(far_sum.astype(jnp.bfloat16), evens_to_next).astype(jnp.float32), far_sum
    )
    even_sum = after(near_sum + far_sum, odd[1])
    even_slab = slab_amplitudes(even_sum, even_energy)

    partner.append(partner_part(after(odd[1], even_sum)))
    odd_products = [products([own], [after(part, even_slab) for part in partner], 0, 0, cols, depth_tile)]
    amp_even = collected(after(even_slab, odd_products[0]))
    partner.append(partner_part(after(odd[2], even_slab)))
    odd_products.append(products([own], partner[2:], 0, 0, cols, depth_tile))
    last.append(last_part(2, last[0], *odd_products))
    odd_products = after(jnp.concatenate(odd_products, axis=1), amp_even, last[0])
    odd_sum = after(spread_sum(odd_products), last[1])
    last.append(last_part(3, odd_sum))
    amp_odd = collected(after(slab_amplitudes(odd_sum, odd_energy), last[2]))

    gamma = density(None, amp_even, amp_odd, early, partner, early_half * (half // wide_tile), wide_tile)
    for part, block in enumerate(last):
        at = (1 - early_half) * (half // tile) + part * (l_cols // tile)
        gamma = density(gamma, amp_even, amp_odd, [block], partner, at, tile)
    return gamma.reshape(occ_rows, slab, cols)


def solution(mesh):
    placed = (P("occ", None, "aux"), P("occ"), P())
    return jax.shard_map(
        per_device, mesh=mesh, in_specs=placed, out_specs=P("occ", None, "aux"), check_vma=False
    )
```

```python
import functools

import jax
import jax.numpy as jnp
from jax import lax
from jax.experimental import pallas as pl
from jax.experimental.pallas import tpu as pltpu
from jax.sharding import PartitionSpec as P

VMEM_BYTES = 24 * 1024 * 1024


def after(value, *earlier):
    return lax.optimization_barrier((value,) + earlier)[0]


IN_VMEM = pl.BlockSpec(memory_space=pltpu.VMEM)


def part(ref, step, size):
    return ref[:, pl.ds(pl.multiple_of(step * size, size), size)]


def joined(arrays, dim):
    return arrays[0] if len(arrays) == 1 else jnp.concatenate(arrays, axis=dim)


def product_kernel(tile, left_ref, *refs):
    right, out_ref, total = refs[:-2], refs[-2], refs[-1]
    total[...] = jnp.zeros_like(total)

    def body(step, carry):
        total[...] += lax.dot_general(
            part(left_ref, step, tile),
            joined([part(ref, step, tile) for ref in right], 0),
            (((1,), (1,)), ((), ())),
            preferred_element_type=jnp.float32,
        )
        return carry

    lax.fori_loop(0, left_ref.shape[1] // tile, body, 0)
    out_ref[...] = total[...].astype(out_ref.dtype)


def products(left, right, tile):
    rows, depth = left.shape
    cols = sum(array.shape[0] for array in right)
    return pl.pallas_call(
        functools.partial(product_kernel, tile),
        out_shape=jax.ShapeDtypeStruct((rows, cols), jnp.bfloat16),
        in_specs=[IN_VMEM] * (1 + len(right)),
        out_specs=IN_VMEM,
        scratch_shapes=[pltpu.VMEM((rows, cols), jnp.float32)],
        compiler_params=pltpu.CompilerParams(vmem_limit_bytes=VMEM_BYTES),
        cost_estimate=pl.CostEstimate(
            flops=2 * rows * cols * depth, bytes_accessed=2 * (rows + cols) * depth, transcendentals=0
        ),
        name="products",
    )(left, *right)


def swapped(x, width):
    rows, cols = x.shape
    r = lax.broadcasted_iota(jnp.int32, x.shape, 0)
    c = lax.broadcasted_iota(jnp.int32, x.shape, 1)
    s = 1
    while s < width:
        below = pltpu.roll(pltpu.roll(x, rows - s, 0), s, 1)
        above = pltpu.roll(pltpu.roll(x, s, 0), cols - s, 1)
        r_bit, c_bit = (r & s) != 0, (c & s) != 0
        x = jnp.where(r_bit == c_bit, x, jnp.where(c_bit, below, above))
        s *= 2
    return x


def amplitude_kernel(width, row_ref, col_ref, *refs):
    x = refs[0][...].astype(jnp.float32)
    for ref in refs[1:-1]:
        x = x + ref[...].astype(jnp.float32)
    refs[-1][...] = ((2.0 * x - swapped(x, width)) / (row_ref[...] + col_ref[...])).astype(refs[-1].dtype)


def amplitudes(terms, row, col, width):
    rows, cols = terms[0].shape
    block = min(rows, 128)
    return pl.pallas_call(
        functools.partial(amplitude_kernel, width),
        out_shape=jax.ShapeDtypeStruct((rows, cols), jnp.bfloat16),
        grid=(rows // block,),
        in_specs=[pl.BlockSpec((block, 1), lambda r: (r, 0)), pl.BlockSpec((1, cols), lambda r: (0, 0))]
        + [pl.BlockSpec((block, cols), lambda r: (r, 0)) for _ in terms],
        out_specs=pl.BlockSpec((block, cols), lambda r: (r, 0)),
        compiler_params=pltpu.CompilerParams(vmem_limit_bytes=VMEM_BYTES),
        cost_estimate=pl.CostEstimate(flops=60 * rows * cols, bytes_accessed=8 * rows * cols, transcendentals=0),
        name="amplitudes",
    )(row, col, *terms)


def tile_density(amp, blocks, step, tile):
    block = joined([part(ref, step, tile) for ref in blocks], 0)
    return jnp.dot(amp, block, preferred_element_type=jnp.float32)


def first_density_kernel(tile, amp_ref, *refs):
    blocks, out_ref = refs[:-1], refs[-1]

    def body(step, carry):
        total = tile_density(amp_ref[...], blocks, step, tile)
        out_ref[:, pl.ds(pl.multiple_of(step * tile, tile), tile)] = total.astype(out_ref.dtype)
        return carry

    lax.fori_loop(0, out_ref.shape[1] // tile, body, 0)


def first_density(amp, blocks, tile):
    rows, cols = amp.shape[0], blocks[0].shape[1]
    return pl.pallas_call(
        functools.partial(first_density_kernel, tile),
        out_shape=jax.ShapeDtypeStruct((rows, cols), jnp.bfloat16),
        in_specs=[IN_VMEM] * (1 + len(blocks)),
        out_specs=IN_VMEM,
        compiler_params=pltpu.CompilerParams(vmem_limit_bytes=VMEM_BYTES),
        cost_estimate=pl.CostEstimate(
            flops=2 * rows * rows * cols, bytes_accessed=4 * rows * cols, transcendentals=0
        ),
        name="first_density",
    )(amp, *blocks)


def last_density_kernel(tile, n_parts, *refs):
    amps, blocks = refs[:n_parts], refs[n_parts:2 * n_parts]
    start_ref, out_ref, amp, buffers, sems = refs[2 * n_parts:]
    amp[...] = joined([ref[...] for ref in amps], 1)
    steps = start_ref.shape[1] // tile

    def copy_out(slot, step):
        columns = pl.ds(pl.multiple_of(step * tile, tile), tile)
        return pltpu.make_async_copy(buffers.at[slot], out_ref.at[:, columns], sems.at[slot])

    for step in range(steps):
        slot = step % 2
        if step >= 2:
            copy_out(slot, step - 2).wait()
        total = tile_density(amp[...], blocks, step, tile) + part(start_ref, step, tile).astype(jnp.float32)
        buffers[slot] = total.astype(buffers.dtype)
        copy_out(slot, step).start()
    for step in range(max(steps - 2, 0), steps):
        copy_out(step % 2, step).wait()


def last_density(amps, blocks, start, tile):
    rows, cols = start.shape
    return pl.pallas_call(
        functools.partial(last_density_kernel, tile, len(amps)),
        out_shape=jax.ShapeDtypeStruct((rows, cols), jnp.bfloat16),
        in_specs=[IN_VMEM] * (2 * len(amps) + 1),
        out_specs=pl.BlockSpec(memory_space=pl.ANY),
        scratch_shapes=[
            pltpu.VMEM((rows, rows), jnp.bfloat16),
            pltpu.VMEM((2, rows, tile), jnp.bfloat16),
            pltpu.SemaphoreType.DMA((2,)),
        ],
        compiler_params=pltpu.CompilerParams(vmem_limit_bytes=VMEM_BYTES),
        cost_estimate=pl.CostEstimate(
            flops=2 * rows * rows * cols, bytes_accessed=6 * rows * cols, transcendentals=0
        ),
        name="last_density",
    )(*amps, *blocks, start)


def per_device(b_factor, occ_energy, virt_energy):
    occ_rows, slab, cols = b_factor.shape
    rows = occ_rows * slab
    n_occ, n_aux = lax.axis_size("occ"), lax.axis_size("aux")
    q = lax.axis_index("aux")
    n_y = n_aux // 2
    y_groups = [list(range(n_y)), list(range(n_y, n_aux))]
    own_rows = rows // n_y
    depth_tile, tile = cols // 6, cols // 8
    large = 3 * rows // 4

    ring = [(i, (i + 1) % n_occ) for i in range(n_occ)]
    two_on = [(i, (i + 2) % n_occ) for i in range(n_occ)]
    other_x = [(i, (i + n_y) % n_aux) for i in range(n_aux)]

    def send(value, pairs=ring):
        return lax.ppermute(value, "occ", pairs)

    def across(value):
        return lax.ppermute(value.astype(jnp.bfloat16), "aux", other_x)

    own = b_factor.reshape(rows, cols)
    near_large, near_small = send(own[:large]), send(own[large:])
    energy = after(occ_energy, near_small)
    energy_near, energy_far = send(energy), send(energy, two_on)
    far_large = send(after(near_large, energy_near, energy_far))

    energy_near, energy_far, own_energy, _ = lax.optimization_barrier(
        (energy_near, energy_far, occ_energy, near_large)
    )
    row = (own_energy[:, None] - virt_energy[None, :]).reshape(rows, 1)
    own_row = lax.dynamic_slice(row, ((q % n_y) * own_rows, 0), (own_rows, 1))
    near_col = (energy_near[:, None] - virt_energy[None, :]).reshape(1, rows)
    far_col = (energy_far[:, None] - virt_energy[None, :]).reshape(1, rows)

    near_products = products(own, [near_large, near_small], depth_tile)
    far_small = send(after(near_small, far_large, near_products))
    amp_near = amplitudes([lax.psum(near_products, "aux")], row, near_col, slab)
    near_density = first_density(amp_near, [near_large, near_small], tile)

    large_parts = lax.all_to_all(
        products(own, [far_large], depth_tile).reshape(n_y, own_rows, large), "aux", 0, 0, axis_index_groups=y_groups
    )
    large_sum = large_parts.astype(jnp.float32).sum(0)
    large_slab = amplitudes([large_sum, across(large_sum)], own_row, far_col[:, :large], slab)
    amp_large = lax.all_to_all(
        jnp.broadcast_to(large_slab, (n_y, own_rows, large)), "aux", 0, 0, axis_index_groups=y_groups
    ).reshape(rows, large)

    small_products = products(own, [after(far_small, near_density)], depth_tile)
    small_parts = lax.all_to_all(
        jnp.broadcast_to(small_products, (n_y, rows, rows - large)), "aux", 0, 0, axis_index_groups=y_groups
    )
    small_sum = small_parts.astype(jnp.float32).sum(0)
    amp_small = amplitudes([small_sum, across(small_sum)], row, far_col[:, large:], slab)

    gamma = last_density([amp_large, amp_small], [far_large, far_small], near_density, tile)
    return gamma.reshape(occ_rows, slab, cols)


def solution(mesh):
    placed = (P("occ", None, "aux"), P("occ"), P())
    return jax.shard_map(
        per_device, mesh=mesh, in_specs=placed, out_specs=P("occ", None, "aux"), check_vma=False
    )
```

```python
import functools

import jax
import jax.numpy as jnp
from jax import lax
from jax.experimental import pallas as pl
from jax.experimental.pallas import tpu as pltpu
from jax.sharding import PartitionSpec as P

VMEM_BYTES = 8 * 1024 * 1024


def after(value, *earlier):
    return lax.optimization_barrier((value,) + earlier)[0]


IN_VMEM = pl.BlockSpec(memory_space=pltpu.VMEM)


def part(ref, step, size):
    return ref[:, pl.ds(pl.multiple_of(step * size, size), size)]


def joined(arrays, dim):
    return arrays[0] if len(arrays) == 1 else jnp.concatenate(arrays, axis=dim)


def product_kernel(tile, left_ref, *refs):
    right, out_ref, total = refs[:-2], refs[-2], refs[-1]
    total[...] = jnp.zeros_like(total)

    def body(step, carry):
        total[...] += lax.dot_general(
            part(left_ref, step, tile),
            joined([part(ref, step, tile) for ref in right], 0),
            (((1,), (1,)), ((), ())),
            preferred_element_type=jnp.float32,
        )
        return carry

    lax.fori_loop(0, left_ref.shape[1] // tile, body, 0)
    out_ref[...] = total[...].astype(out_ref.dtype)


def products(left, right, tile):
    rows, depth = left.shape
    cols = sum(array.shape[0] for array in right)
    return pl.pallas_call(
        functools.partial(product_kernel, tile),
        out_shape=jax.ShapeDtypeStruct((rows, cols), jnp.bfloat16),
        in_specs=[IN_VMEM] * (1 + len(right)),
        out_specs=IN_VMEM,
        scratch_shapes=[pltpu.VMEM((rows, cols), jnp.float32)],
        compiler_params=pltpu.CompilerParams(vmem_limit_bytes=VMEM_BYTES),
        cost_estimate=pl.CostEstimate(
            flops=2 * rows * cols * depth, bytes_accessed=2 * (rows + cols) * depth, transcendentals=0
        ),
        name="products",
    )(left, *right)


def swapped(x, width):
    rows, cols = x.shape
    r = lax.broadcasted_iota(jnp.int32, x.shape, 0)
    c = lax.broadcasted_iota(jnp.int32, x.shape, 1)
    s = 1
    while s < width:
        below = pltpu.roll(pltpu.roll(x, rows - s, 0), s, 1)
        above = pltpu.roll(pltpu.roll(x, s, 0), cols - s, 1)
        r_bit, c_bit = (r & s) != 0, (c & s) != 0
        x = jnp.where(r_bit == c_bit, x, jnp.where(c_bit, below, above))
        s *= 2
    return x


def amplitude_kernel(width, parts_ref, row_ref, col_ref, out_ref):
    x = parts_ref[0].astype(jnp.float32)
    for part_at in range(1, parts_ref.shape[0]):
        x = x + parts_ref[part_at].astype(jnp.float32)
    result = ((2.0 * x - swapped(x, width)) / (row_ref[...] + col_ref[...])).astype(out_ref.dtype)
    for copy_at in range(out_ref.shape[0]):
        out_ref[copy_at] = result


def amplitudes(parts, row, col, width, copies):
    _, rows, cols = parts.shape
    return pl.pallas_call(
        functools.partial(amplitude_kernel, width),
        out_shape=jax.ShapeDtypeStruct((copies, rows, cols), jnp.bfloat16),
        in_specs=[IN_VMEM] * 3,
        out_specs=IN_VMEM,
        compiler_params=pltpu.CompilerParams(vmem_limit_bytes=VMEM_BYTES),
        cost_estimate=pl.CostEstimate(
            flops=60 * rows * cols, bytes_accessed=2 * parts.size, transcendentals=0
        ),
        name="amplitudes",
    )(parts, row, col)


def tile_density(amp, blocks, step, tile):
    block = joined([part(ref, step, tile) for ref in blocks], 0)
    return jnp.dot(amp, block, preferred_element_type=jnp.float32)


def first_density_kernel(tile, amp_ref, *refs):
    blocks, out_ref = refs[:-1], refs[-1]

    def body(step, carry):
        total = tile_density(amp_ref[...], blocks, step, tile)
        out_ref[:, pl.ds(pl.multiple_of(step * tile, tile), tile)] = total.astype(out_ref.dtype)
        return carry

    lax.fori_loop(0, out_ref.shape[1] // tile, body, 0)


def first_density(amp, blocks, tile):
    rows, cols = amp.shape[0], blocks[0].shape[1]
    return pl.pallas_call(
        functools.partial(first_density_kernel, tile),
        out_shape=jax.ShapeDtypeStruct((rows, cols), jnp.bfloat16),
        in_specs=[IN_VMEM] * (1 + len(blocks)),
        out_specs=IN_VMEM,
        compiler_params=pltpu.CompilerParams(vmem_limit_bytes=VMEM_BYTES),
        cost_estimate=pl.CostEstimate(
            flops=2 * rows * rows * cols, bytes_accessed=4 * rows * cols, transcendentals=0
        ),
        name="first_density",
    )(amp, *blocks)


def last_density_kernel(tile, n_blocks, amp_ref, *refs):
    blocks = refs[:n_blocks]
    start_ref, out_ref, buffers, sems = refs[n_blocks:]
    steps = start_ref.shape[1] // tile

    def copy_out(slot, step):
        columns = pl.ds(step * tile, tile)
        return pltpu.make_async_copy(buffers.at[slot], out_ref.at[:, columns], sems.at[slot])

    for step in range(steps):
        slot = step % 2
        if step >= 2:
            copy_out(slot, step - 2).wait()
        total = tile_density(amp_ref[...], blocks, step, tile) + part(start_ref, step, tile).astype(jnp.float32)
        buffers[slot] = total.astype(buffers.dtype)
        copy_out(slot, step).start()
    for step in range(max(steps - 2, 0), steps):
        copy_out(step % 2, step).wait()


def last_density(amp, blocks, start, tile):
    rows, cols = start.shape
    return pl.pallas_call(
        functools.partial(last_density_kernel, tile, len(blocks)),
        out_shape=jax.ShapeDtypeStruct((rows, cols), jnp.bfloat16),
        in_specs=[IN_VMEM] * (2 + len(blocks)),
        out_specs=pl.BlockSpec(memory_space=pl.ANY),
        scratch_shapes=[pltpu.VMEM((2, rows, tile), jnp.bfloat16), pltpu.SemaphoreType.DMA((2,))],
        compiler_params=pltpu.CompilerParams(vmem_limit_bytes=VMEM_BYTES),
        cost_estimate=pl.CostEstimate(
            flops=2 * rows * rows * cols, bytes_accessed=6 * rows * cols, transcendentals=0
        ),
        name="last_density",
    )(amp, *blocks, start)


def per_device(b_factor, occ_energy, virt_energy):
    occ_rows, slab, cols = b_factor.shape
    rows = occ_rows * slab
    n_occ, n_aux = lax.axis_size("occ"), lax.axis_size("aux")
    q = lax.axis_index("aux")
    n_y = n_aux // 2
    y_groups = [list(range(n_y)), list(range(n_y, n_aux))]
    x_groups = [[i, i + n_y] for i in range(n_y)]
    depth_tile, tile = cols // 6, cols // 8
    large = 3 * rows // 4

    def send(value, by=1):
        return lax.ppermute(value, "occ", [(i, (i + by) % n_occ) for i in range(n_occ)])

    def exchanged(value, groups):
        return lax.all_to_all(value, "aux", 0, 0, axis_index_groups=groups)

    def repeated(value, groups):
        return exchanged(jnp.broadcast_to(value, (len(groups[0]),) + value.shape), groups)

    def total(parts):
        return parts.astype(jnp.float32).sum(0).astype(jnp.bfloat16)

    own = b_factor.reshape(rows, cols)
    energy_near, energy_far = send(occ_energy), send(occ_energy, 2)
    near = send(own)
    ready = after(near, energy_near, energy_far)
    large_rows = ready[:large]
    far_large = send(large_rows)
    far_small = send(after(ready, large_rows)[large:])

    row = (occ_energy[:, None] - virt_energy[None, :]).reshape(rows, 1)
    near_col = (energy_near[:, None] - virt_energy[None, :]).reshape(1, rows)
    far_col = (energy_far[:, None] - virt_energy[None, :]).reshape(1, rows)

    def share(index, size):
        return lax.dynamic_slice(row, (index * size, 0), (size, 1))

    near_products = products(own, [near], depth_tile)
    y_sum = total(exchanged(near_products.reshape(n_y, rows // n_y, rows), y_groups))
    near_parts = repeated(y_sum, x_groups)
    near_slab = amplitudes(near_parts, share(q % n_y, rows // n_y), near_col, slab, n_y)
    amp_near = exchanged(near_slab, y_groups).reshape(rows, rows)
    near_density = first_density(amp_near, [near], tile)

    large_products = products(own, [after(far_large, near_density)], depth_tile)
    small_products = products(own, [after(far_small, large_products)], depth_tile)
    far_products = jnp.concatenate([large_products, small_products], axis=1)
    far_parts = lax.all_to_all(far_products.reshape(n_aux, rows // n_aux, rows), "aux", 0, 0)
    far_slab = amplitudes(far_parts, share(q, rows // n_aux), far_col, slab, n_aux)
    amp_far = lax.all_to_all(far_slab, "aux", 0, 0).reshape(rows, rows)
    gamma = last_density(amp_far, [far_large, far_small], near_density, tile)
    return gamma.reshape(occ_rows, slab, cols)


def solution(mesh):
    placed = (P("occ", None, "aux"), P("occ"), P())
    return jax.shard_map(
        per_device, mesh=mesh, in_specs=placed, out_specs=P("occ", None, "aux"), check_vma=False
    )
```

```python
import functools

import jax
import jax.numpy as jnp
from jax import lax
from jax.experimental import pallas as pl
from jax.experimental.pallas import tpu as pltpu
from jax.sharding import PartitionSpec as P

VMEM_BYTES = 8 * 1024 * 1024


def after(value, *earlier):
    return lax.optimization_barrier((value,) + earlier)[0]


IN_VMEM = pl.BlockSpec(memory_space=pltpu.VMEM)


def part(ref, step, size):
    return ref[:, pl.ds(pl.multiple_of(step * size, size), size)]


def joined(arrays, dim):
    return arrays[0] if len(arrays) == 1 else jnp.concatenate(arrays, axis=dim)


def product_kernel(tile, n_right, left_ref, *refs):
    right, before, out_ref, total = refs[:n_right], refs[n_right:-2], refs[-2], refs[-1]
    total[...] = jnp.zeros_like(total)

    def body(step, carry):
        total[...] += lax.dot_general(
            part(left_ref, step, tile),
            joined([part(ref, step, tile) for ref in right], 0),
            (((1,), (1,)), ((), ())),
            preferred_element_type=jnp.float32,
        )
        return carry

    lax.fori_loop(0, left_ref.shape[1] // tile, body, 0)
    out_ref[...] = joined([ref[...] for ref in before] + [total[...].astype(out_ref.dtype)], 1)


def products(left, right, tile, before=()):
    rows, depth = left.shape
    cols = sum(array.shape[0] for array in right)
    width = cols + sum(array.shape[1] for array in before)
    return pl.pallas_call(
        functools.partial(product_kernel, tile, len(right)),
        out_shape=jax.ShapeDtypeStruct((rows, width), jnp.bfloat16),
        in_specs=[IN_VMEM] * (1 + len(right) + len(before)),
        out_specs=IN_VMEM,
        scratch_shapes=[pltpu.VMEM((rows, cols), jnp.float32)],
        compiler_params=pltpu.CompilerParams(vmem_limit_bytes=VMEM_BYTES),
        cost_estimate=pl.CostEstimate(
            flops=2 * rows * cols * depth, bytes_accessed=2 * (rows + cols) * depth, transcendentals=0
        ),
        name="products",
    )(left, *right, *before)


def swapped(x, width):
    rows, cols = x.shape
    r = lax.broadcasted_iota(jnp.int32, x.shape, 0)
    c = lax.broadcasted_iota(jnp.int32, x.shape, 1)
    s = 1
    while s < width:
        below = pltpu.roll(pltpu.roll(x, rows - s, 0), s, 1)
        above = pltpu.roll(pltpu.roll(x, s, 0), cols - s, 1)
        r_bit, c_bit = (r & s) != 0, (c & s) != 0
        x = jnp.where(r_bit == c_bit, x, jnp.where(c_bit, below, above))
        s *= 2
    return x


def amplitude_kernel(width, parts_ref, row_ref, col_ref, out_ref):
    x = parts_ref[0].astype(jnp.float32)
    for part_at in range(1, parts_ref.shape[0]):
        x = x + parts_ref[part_at].astype(jnp.float32)
    result = ((2.0 * x - swapped(x, width)) / (row_ref[...] + col_ref[...])).astype(out_ref.dtype)
    for copy_at in range(out_ref.shape[0]):
        out_ref[copy_at] = result


def amplitudes(parts, row, col, width, copies):
    _, rows, cols = parts.shape
    return pl.pallas_call(
        functools.partial(amplitude_kernel, width),
        out_shape=jax.ShapeDtypeStruct((copies, rows, cols), jnp.bfloat16),
        in_specs=[IN_VMEM] * 3,
        out_specs=IN_VMEM,
        compiler_params=pltpu.CompilerParams(vmem_limit_bytes=VMEM_BYTES),
        cost_estimate=pl.CostEstimate(
            flops=60 * rows * cols, bytes_accessed=2 * parts.size, transcendentals=0
        ),
        name="amplitudes",
    )(parts, row, col)


def tile_density(amp, blocks, step, tile):
    block = joined([part(ref, step, tile) for ref in blocks], 0)
    return jnp.dot(amp, block, preferred_element_type=jnp.float32)


def first_density_kernel(tile, amp_ref, *refs):
    blocks, out_ref = refs[:-1], refs[-1]

    def body(step, carry):
        total = tile_density(amp_ref[...], blocks, step, tile)
        out_ref[:, pl.ds(pl.multiple_of(step * tile, tile), tile)] = total.astype(out_ref.dtype)
        return carry

    lax.fori_loop(0, out_ref.shape[1] // tile, body, 0)


def first_density(amp, blocks, tile):
    rows, cols = amp.shape[0], blocks[0].shape[1]
    return pl.pallas_call(
        functools.partial(first_density_kernel, tile),
        out_shape=jax.ShapeDtypeStruct((rows, cols), jnp.bfloat16),
        in_specs=[IN_VMEM] * (1 + len(blocks)),
        out_specs=IN_VMEM,
        compiler_params=pltpu.CompilerParams(vmem_limit_bytes=VMEM_BYTES),
        cost_estimate=pl.CostEstimate(
            flops=2 * rows * rows * cols, bytes_accessed=4 * rows * cols, transcendentals=0
        ),
        name="first_density",
    )(amp, *blocks)


def last_density_kernel(amp_ref, *refs):
    blocks, start_ref, out_ref = refs[:-2], refs[-2], refs[-1]
    total = jnp.dot(amp_ref[...], joined([ref[...] for ref in blocks], 0), preferred_element_type=jnp.float32)
    out_ref[...] = (total + start_ref[...].astype(jnp.float32)).astype(out_ref.dtype)


def last_density(amp, blocks, start, tile):
    rows, cols = start.shape
    return pl.pallas_call(
        last_density_kernel,
        out_shape=jax.ShapeDtypeStruct((rows, cols), jnp.bfloat16),
        grid=(cols // tile,),
        in_specs=[pl.BlockSpec(amp.shape, lambda c: (0, 0))]
        + [pl.BlockSpec((array.shape[0], tile), lambda c: (0, c)) for array in (*blocks, start)],
        out_specs=pl.BlockSpec((rows, tile), lambda c: (0, c)),
        compiler_params=pltpu.CompilerParams(vmem_limit_bytes=2 * VMEM_BYTES),
        cost_estimate=pl.CostEstimate(
            flops=2 * rows * rows * cols, bytes_accessed=6 * rows * cols, transcendentals=0
        ),
        name="last_density",
    )(amp, *blocks, start)


def per_device(b_factor, occ_energy, virt_energy):
    occ_rows, slab, cols = b_factor.shape
    rows = occ_rows * slab
    n_occ, n_aux = lax.axis_size("occ"), lax.axis_size("aux")
    q = lax.axis_index("aux")
    n_y = n_aux // 2
    y_groups = [list(range(n_y)), list(range(n_y, n_aux))]
    x_groups = [[i, i + n_y] for i in range(n_y)]
    depth_tile, tile = cols // 6, cols // 8
    far_rows = [slice(0, 3 * rows // 8), slice(3 * rows // 8, 3 * rows // 4), slice(3 * rows // 4, rows)]

    def send(value, by=1):
        return lax.ppermute(value, "occ", [(i, (i + by) % n_occ) for i in range(n_occ)])

    def exchanged(value, groups):
        return lax.all_to_all(value, "aux", 0, 0, axis_index_groups=groups)

    def repeated(value, groups):
        return exchanged(jnp.broadcast_to(value, (len(groups[0]),) + value.shape), groups)

    def total(parts):
        return parts.astype(jnp.float32).sum(0).astype(jnp.bfloat16)

    own = b_factor.reshape(rows, cols)
    energy_near, energy_far = send(occ_energy), send(occ_energy, 2)
    near = send(own)
    ready = after(near, energy_near, energy_far)
    first_rows = ready[far_rows[0]]
    far = [send(first_rows)]

    row = (occ_energy[:, None] - virt_energy[None, :]).reshape(rows, 1)
    near_col = (energy_near[:, None] - virt_energy[None, :]).reshape(1, rows)
    far_col = (energy_far[:, None] - virt_energy[None, :]).reshape(1, rows)

    def share(index, size):
        return lax.dynamic_slice(row, (index * size, 0), (size, 1))

    near_products = products(own, [after(near, first_rows)], depth_tile)
    y_sum = total(exchanged(near_products.reshape(n_y, rows // n_y, rows), y_groups))
    near_parts = repeated(y_sum, x_groups)
    ready = after(ready, near_parts, far[0])
    far += [send(ready[far_rows[1]]), send(ready[far_rows[2]])]
    near_slab = amplitudes(near_parts, share(q % n_y, rows // n_y), near_col, slab, n_y)
    amp_near = exchanged(near_slab, y_groups).reshape(rows, rows)
    near_density = first_density(amp_near, [near], tile)

    first_products = products(own, [far[0], after(far[1], near_density)], depth_tile)
    far_products = products(own, [after(far[2], first_products)], depth_tile, (first_products,))
    far_parts = lax.all_to_all(far_products.reshape(n_aux, rows // n_aux, rows), "aux", 0, 0)
    far_slab = amplitudes(far_parts, share(q, rows // n_aux), far_col, slab, n_aux)
    amp_far = lax.all_to_all(far_slab, "aux", 0, 0).reshape(rows, rows)
    gamma = last_density(amp_far, far, near_density, tile)
    return gamma.reshape(occ_rows, slab, cols)


def solution(mesh):
    placed = (P("occ", None, "aux"), P("occ"), P())
    return jax.shard_map(
        per_device, mesh=mesh, in_specs=placed, out_specs=P("occ", None, "aux"), check_vma=False
    )
```

```python
import functools

import jax
import jax.numpy as jnp
from jax import lax
from jax.experimental import pallas as pl
from jax.experimental.pallas import tpu as pltpu
from jax.sharding import PartitionSpec as P

VMEM_BYTES = 8 * 1024 * 1024


def after(value, *earlier):
    return lax.optimization_barrier((value,) + earlier)[0]


IN_VMEM = pl.BlockSpec(memory_space=pltpu.VMEM)


def part(ref, step, size):
    return ref[:, pl.ds(pl.multiple_of(step * size, size), size)]


def joined(arrays, dim):
    return arrays[0] if len(arrays) == 1 else jnp.concatenate(arrays, axis=dim)


def product_kernel(tile, left_ref, *refs):
    right, out_ref, total = refs[:-2], refs[-2], refs[-1]
    total[...] = jnp.zeros_like(total)

    def body(step, carry):
        total[...] += lax.dot_general(
            part(left_ref, step, tile),
            joined([part(ref, step, tile) for ref in right], 0),
            (((1,), (1,)), ((), ())),
            preferred_element_type=jnp.float32,
        )
        return carry

    lax.fori_loop(0, left_ref.shape[1] // tile, body, 0)
    out_ref[...] = total[...].astype(out_ref.dtype)


def products(left, right, tile):
    rows, depth = left.shape
    cols = sum(array.shape[0] for array in right)
    return pl.pallas_call(
        functools.partial(product_kernel, tile),
        out_shape=jax.ShapeDtypeStruct((rows, cols), jnp.bfloat16),
        in_specs=[IN_VMEM] * (1 + len(right)),
        out_specs=IN_VMEM,
        scratch_shapes=[pltpu.VMEM((rows, cols), jnp.float32)],
        compiler_params=pltpu.CompilerParams(vmem_limit_bytes=VMEM_BYTES),
        cost_estimate=pl.CostEstimate(
            flops=2 * rows * cols * depth, bytes_accessed=2 * (rows + cols) * depth, transcendentals=0
        ),
        name="products",
    )(left, *right)


def swapped(x, width):
    rows, cols = x.shape
    r = lax.broadcasted_iota(jnp.int32, x.shape, 0)
    c = lax.broadcasted_iota(jnp.int32, x.shape, 1)
    s = 1
    while s < width:
        below = pltpu.roll(pltpu.roll(x, rows - s, 0), s, 1)
        above = pltpu.roll(pltpu.roll(x, s, 0), cols - s, 1)
        r_bit, c_bit = (r & s) != 0, (c & s) != 0
        x = jnp.where(r_bit == c_bit, x, jnp.where(c_bit, below, above))
        s *= 2
    return x


def amplitude_kernel(width, parts_ref, row_ref, col_ref, out_ref):
    x = parts_ref[0].astype(jnp.float32)
    for part_at in range(1, parts_ref.shape[0]):
        x = x + parts_ref[part_at].astype(jnp.float32)
    result = ((2.0 * x - swapped(x, width)) / (row_ref[...] + col_ref[...])).astype(out_ref.dtype)
    for copy_at in range(out_ref.shape[0]):
        out_ref[copy_at] = result


def amplitudes(parts, row, col, width, copies):
    _, rows, cols = parts.shape
    return pl.pallas_call(
        functools.partial(amplitude_kernel, width),
        out_shape=jax.ShapeDtypeStruct((copies, rows, cols), jnp.bfloat16),
        in_specs=[IN_VMEM] * 3,
        out_specs=IN_VMEM,
        compiler_params=pltpu.CompilerParams(vmem_limit_bytes=VMEM_BYTES),
        cost_estimate=pl.CostEstimate(
            flops=60 * rows * cols, bytes_accessed=2 * parts.size, transcendentals=0
        ),
        name="amplitudes",
    )(parts, row, col)


def tile_density(amp, blocks, step, tile):
    block = joined([part(ref, step, tile) for ref in blocks], 0)
    return jnp.dot(amp, block, preferred_element_type=jnp.float32)


def first_density_kernel(tile, amp_ref, *refs):
    blocks, out_ref = refs[:-1], refs[-1]

    def body(step, carry):
        total = tile_density(amp_ref[...], blocks, step, tile)
        out_ref[:, pl.ds(pl.multiple_of(step * tile, tile), tile)] = total.astype(out_ref.dtype)
        return carry

    lax.fori_loop(0, out_ref.shape[1] // tile, body, 0)


def first_density(amp, blocks, tile):
    rows, cols = amp.shape[0], blocks[0].shape[1]
    return pl.pallas_call(
        functools.partial(first_density_kernel, tile),
        out_shape=jax.ShapeDtypeStruct((rows, cols), jnp.bfloat16),
        in_specs=[IN_VMEM] * (1 + len(blocks)),
        out_specs=IN_VMEM,
        compiler_params=pltpu.CompilerParams(vmem_limit_bytes=VMEM_BYTES),
        cost_estimate=pl.CostEstimate(
            flops=2 * rows * rows * cols, bytes_accessed=4 * rows * cols, transcendentals=0
        ),
        name="first_density",
    )(amp, *blocks)


def last_density_kernel(amp_ref, *refs):
    blocks, start_ref, out_ref = refs[:-2], refs[-2], refs[-1]
    total = jnp.dot(amp_ref[...], joined([ref[...] for ref in blocks], 0), preferred_element_type=jnp.float32)
    out_ref[...] = (total + start_ref[...].astype(jnp.float32)).astype(out_ref.dtype)


def last_density(amp, blocks, start, tile):
    rows, cols = start.shape
    return pl.pallas_call(
        last_density_kernel,
        out_shape=jax.ShapeDtypeStruct((rows, cols), jnp.bfloat16),
        grid=(cols // tile,),
        in_specs=[pl.BlockSpec(amp.shape, lambda c: (0, 0))]
        + [pl.BlockSpec((array.shape[0], tile), lambda c: (0, c)) for array in (*blocks, start)],
        out_specs=pl.BlockSpec((rows, tile), lambda c: (0, c)),
        compiler_params=pltpu.CompilerParams(vmem_limit_bytes=7 * VMEM_BYTES),
        cost_estimate=pl.CostEstimate(
            flops=2 * rows * rows * cols, bytes_accessed=6 * rows * cols, transcendentals=0
        ),
        name="last_density",
    )(amp, *blocks, start)


def per_device(b_factor, occ_energy, virt_energy):
    occ_rows, slab, cols = b_factor.shape
    rows = occ_rows * slab
    n_occ, n_aux = lax.axis_size("occ"), lax.axis_size("aux")
    q = lax.axis_index("aux")
    n_y = n_aux // 2
    y_groups = [list(range(n_y)), list(range(n_y, n_aux))]
    x_groups = [[i, i + n_y] for i in range(n_y)]
    depth_tile, tile = cols // 6, cols // 8
    second, third = 15 * rows // 32, 3 * rows // 4

    def send(value, by=1):
        return lax.ppermute(value, "occ", [(i, (i + by) % n_occ) for i in range(n_occ)])

    def exchanged(value, groups):
        return lax.all_to_all(value, "aux", 0, 0, axis_index_groups=groups)

    def repeated(value, groups):
        return exchanged(jnp.broadcast_to(value, (len(groups[0]),) + value.shape), groups)

    def total(parts):
        return parts.astype(jnp.float32).sum(0).astype(jnp.bfloat16)

    own = b_factor.reshape(rows, cols)
    energy_near, energy_far = send(occ_energy), send(occ_energy, 2)
    near = send(own)
    ready = after(near, energy_near, energy_far)
    first_rows = ready[:second]
    far = [send(first_rows)]
    later = after(ready, first_rows)
    later_rows = [later[second:third], later[third:]]

    row = (occ_energy[:, None] - virt_energy[None, :]).reshape(rows, 1)
    near_col = (energy_near[:, None] - virt_energy[None, :]).reshape(1, rows)
    far_col = (energy_far[:, None] - virt_energy[None, :]).reshape(1, rows)

    def share(index, size):
        return lax.dynamic_slice(row, (index * size, 0), (size, 1))

    near_products = products(own, [after(near, *later_rows)], depth_tile)
    y_sum = total(exchanged(near_products.reshape(n_y, rows // n_y, rows), y_groups))
    near_parts = repeated(y_sum, x_groups)
    far += [send(after(chunk, near_parts, far[0])) for chunk in later_rows]
    near_slab = amplitudes(near_parts, share(q % n_y, rows // n_y), near_col, slab, n_y)
    amp_near = exchanged(near_slab, y_groups).reshape(rows, rows)
    near_density = first_density(amp_near, [near], tile)

    first_products = products(own, [far[0], after(far[1], near_density)], depth_tile)
    last_products = products(own, [after(far[2], first_products)], depth_tile)
    far_products = jnp.concatenate([first_products, last_products], axis=1)
    far_parts = lax.all_to_all(far_products.reshape(n_aux, rows // n_aux, rows), "aux", 0, 0)
    far_slab = amplitudes(far_parts, share(q, rows // n_aux), far_col, slab, n_aux)
    amp_far = lax.all_to_all(far_slab, "aux", 0, 0).reshape(rows, rows)
    gamma = last_density(amp_far, far, near_density, tile)
    return gamma.reshape(occ_rows, slab, cols)


def solution(mesh):
    placed = (P("occ", None, "aux"), P("occ"), P())
    return jax.shard_map(
        per_device, mesh=mesh, in_specs=placed, out_specs=P("occ", None, "aux"), check_vma=False
    )
```

```python
import functools

import jax
import jax.numpy as jnp
from jax import lax
from jax.experimental import pallas as pl
from jax.experimental.pallas import tpu as pltpu
from jax.sharding import PartitionSpec as P

VMEM_BYTES = 8 * 1024 * 1024


def after(value, *earlier):
    return lax.optimization_barrier((value,) + earlier)[0]


IN_VMEM = pl.BlockSpec(memory_space=pltpu.VMEM)


def part(ref, step, size):
    return ref[:, pl.ds(pl.multiple_of(step * size, size), size)]


def joined(arrays, dim):
    return arrays[0] if len(arrays) == 1 else jnp.concatenate(arrays, axis=dim)


def product_kernel(tile, n_sources, *refs):
    sources, out_ref = refs[:n_sources], refs[n_sources]
    buffers, total, sems = refs[n_sources + 1:-2], refs[-2], refs[-1]
    steps = buffers[0].shape[1] // tile

    def copy_in(at, step):
        columns = pl.ds(step * tile, tile)
        return pltpu.make_async_copy(sources[at].at[:, columns], buffers[at].at[:, columns], sems.at[at, step])

    for step in range(steps):
        for at in range(n_sources):
            copy_in(at, step).start()
    for step in range(steps):
        for at in range(n_sources):
            copy_in(at, step).wait()
        columns = pl.ds(step * tile, tile)
        term = lax.dot_general(
            buffers[0][:, columns],
            joined([ref[:, columns] for ref in buffers[1:]], 0),
            (((1,), (1,)), ((), ())),
            preferred_element_type=jnp.float32,
        )
        total[...] = term if step == 0 else total[...] + term
    out_ref[...] = total[...].astype(out_ref.dtype)


def products(left, right, tile):
    rows, depth = left.shape
    cols = sum(array.shape[0] for array in right)
    sources = (left, *right)
    return pl.pallas_call(
        functools.partial(product_kernel, tile, len(sources)),
        out_shape=jax.ShapeDtypeStruct((rows, cols), jnp.bfloat16),
        in_specs=[pl.BlockSpec(memory_space=pl.ANY)] * len(sources),
        out_specs=IN_VMEM,
        scratch_shapes=[pltpu.VMEM(array.shape, jnp.bfloat16) for array in sources]
        + [pltpu.VMEM((rows, cols), jnp.float32), pltpu.SemaphoreType.DMA((len(sources), depth // tile))],
        compiler_params=pltpu.CompilerParams(vmem_limit_bytes=3 * VMEM_BYTES),
        cost_estimate=pl.CostEstimate(
            flops=2 * rows * cols * depth, bytes_accessed=2 * (rows + cols) * depth, transcendentals=0
        ),
        name="products",
    )(*sources)


def swapped(x, width):
    rows, cols = x.shape
    r = lax.broadcasted_iota(jnp.int32, x.shape, 0)
    c = lax.broadcasted_iota(jnp.int32, x.shape, 1)
    s = 1
    while s < width:
        below = pltpu.roll(pltpu.roll(x, rows - s, 0), s, 1)
        above = pltpu.roll(pltpu.roll(x, s, 0), cols - s, 1)
        r_bit, c_bit = (r & s) != 0, (c & s) != 0
        x = jnp.where(r_bit == c_bit, x, jnp.where(c_bit, below, above))
        s *= 2
    return x


def amplitude_kernel(width, parts_ref, row_ref, col_ref, out_ref):
    x = parts_ref[0].astype(jnp.float32)
    for part_at in range(1, parts_ref.shape[0]):
        x = x + parts_ref[part_at].astype(jnp.float32)
    result = ((2.0 * x - swapped(x, width)) / (row_ref[...] + col_ref[...])).astype(out_ref.dtype)
    for copy_at in range(out_ref.shape[0]):
        out_ref[copy_at] = result


def amplitudes(parts, row, col, width, copies):
    _, rows, cols = parts.shape
    return pl.pallas_call(
        functools.partial(amplitude_kernel, width),
        out_shape=jax.ShapeDtypeStruct((copies, rows, cols), jnp.bfloat16),
        in_specs=[IN_VMEM] * 3,
        out_specs=IN_VMEM,
        compiler_params=pltpu.CompilerParams(vmem_limit_bytes=VMEM_BYTES),
        cost_estimate=pl.CostEstimate(
            flops=60 * rows * cols, bytes_accessed=2 * parts.size, transcendentals=0
        ),
        name="amplitudes",
    )(parts, row, col)


def tile_density(amp, blocks, step, tile):
    block = joined([part(ref, step, tile) for ref in blocks], 0)
    return jnp.dot(amp, block, preferred_element_type=jnp.float32)


def first_density_kernel(tile, amp_ref, *refs):
    blocks, out_ref = refs[:-1], refs[-1]

    def body(step, carry):
        total = tile_density(amp_ref[...], blocks, step, tile)
        out_ref[:, pl.ds(pl.multiple_of(step * tile, tile), tile)] = total.astype(out_ref.dtype)
        return carry

    lax.fori_loop(0, out_ref.shape[1] // tile, body, 0)


def first_density(amp, blocks, tile):
    rows, cols = amp.shape[0], blocks[0].shape[1]
    return pl.pallas_call(
        functools.partial(first_density_kernel, tile),
        out_shape=jax.ShapeDtypeStruct((rows, cols), jnp.bfloat16),
        in_specs=[IN_VMEM] * (1 + len(blocks)),
        out_specs=IN_VMEM,
        compiler_params=pltpu.CompilerParams(vmem_limit_bytes=VMEM_BYTES),
        cost_estimate=pl.CostEstimate(
            flops=2 * rows * rows * cols, bytes_accessed=4 * rows * cols, transcendentals=0
        ),
        name="first_density",
    )(amp, *blocks)


def last_density_kernel(tile, n_blocks, *refs):
    sources, out_ref = refs[:n_blocks + 2], refs[n_blocks + 2]
    buffers, out_buffer = refs[n_blocks + 3:2 * n_blocks + 5], refs[2 * n_blocks + 5]
    amp_sem, in_sems, out_sems = refs[2 * n_blocks + 6:]
    amp, blocks, start = buffers[0], buffers[1:-1], buffers[-1]
    steps = start.shape[1] // tile

    def columns(step):
        return pl.ds(step * tile, tile)

    def copy_in(at, step):
        return pltpu.make_async_copy(
            sources[at].at[:, columns(step)], buffers[at].at[:, columns(step)], in_sems.at[at - 1, step]
        )

    def copy_out(step):
        return pltpu.make_async_copy(out_buffer.at[:, columns(step)], out_ref.at[:, columns(step)], out_sems.at[step])

    copy_amp = pltpu.make_async_copy(sources[0], amp, amp_sem)
    copy_amp.start()
    for step in range(steps):
        for at in range(1, n_blocks + 2):
            copy_in(at, step).start()
    copy_amp.wait()
    for step in range(steps):
        for at in range(1, n_blocks + 2):
            copy_in(at, step).wait()
        total = jnp.dot(
            amp[...], joined([ref[:, columns(step)] for ref in blocks], 0), preferred_element_type=jnp.float32
        )
        out_buffer[:, columns(step)] = (total + start[:, columns(step)].astype(jnp.float32)).astype(out_buffer.dtype)
        copy_out(step).start()
    for step in range(steps):
        copy_out(step).wait()


def last_density(amp, blocks, start, tile):
    rows, cols = start.shape
    sources = (amp, *blocks, start)
    in_hbm = pl.BlockSpec(memory_space=pl.ANY)
    return pl.pallas_call(
        functools.partial(last_density_kernel, tile, len(blocks)),
        out_shape=jax.ShapeDtypeStruct((rows, cols), jnp.bfloat16),
        in_specs=[in_hbm] * len(sources),
        out_specs=in_hbm,
        scratch_shapes=[pltpu.VMEM(array.shape, jnp.bfloat16) for array in sources]
        + [
            pltpu.VMEM((rows, cols), jnp.bfloat16),
            pltpu.SemaphoreType.DMA,
            pltpu.SemaphoreType.DMA((len(blocks) + 1, cols // tile)),
            pltpu.SemaphoreType.DMA((cols // tile,)),
        ],
        compiler_params=pltpu.CompilerParams(vmem_limit_bytes=7 * VMEM_BYTES),
        cost_estimate=pl.CostEstimate(
            flops=2 * rows * rows * cols, bytes_accessed=6 * rows * cols, transcendentals=0
        ),
        name="last_density",
    )(*sources)


def per_device(b_factor, occ_energy, virt_energy):
    occ_rows, slab, cols = b_factor.shape
    rows = occ_rows * slab
    n_occ, n_aux = lax.axis_size("occ"), lax.axis_size("aux")
    q = lax.axis_index("aux")
    n_y = n_aux // 2
    y_groups = [list(range(n_y)), list(range(n_y, n_aux))]
    x_groups = [[i, i + n_y] for i in range(n_y)]
    depth_tile, tile = cols // 6, cols // 8
    second, third = 15 * rows // 32, 3 * rows // 4

    def send(value, by=1):
        return lax.ppermute(value, "occ", [(i, (i + by) % n_occ) for i in range(n_occ)])

    def exchanged(value, groups):
        return lax.all_to_all(value, "aux", 0, 0, axis_index_groups=groups)

    def repeated(value, groups):
        return exchanged(jnp.broadcast_to(value, (len(groups[0]),) + value.shape), groups)

    def total(parts):
        return parts.astype(jnp.float32).sum(0).astype(jnp.bfloat16)

    own = b_factor.reshape(rows, cols)
    energy_near, energy_far = send(occ_energy), send(occ_energy, 2)
    near = send(own)
    ready = after(near, energy_near, energy_far)
    first_rows = ready[:second]
    far = [send(first_rows)]
    later = after(ready, first_rows)
    later_rows = [later[second:third], later[third:]]

    row = (occ_energy[:, None] - virt_energy[None, :]).reshape(rows, 1)
    near_col = (energy_near[:, None] - virt_energy[None, :]).reshape(1, rows)
    far_col = (energy_far[:, None] - virt_energy[None, :]).reshape(1, rows)

    def share(index, size):
        return lax.dynamic_slice(row, (index * size, 0), (size, 1))

    near_products = products(own, [after(near, *later_rows)], depth_tile)
    y_sum = total(exchanged(near_products.reshape(n_y, rows // n_y, rows), y_groups))
    near_parts = repeated(y_sum, x_groups)
    far += [send(after(chunk, near_parts, far[0])) for chunk in later_rows]
    near_slab = amplitudes(near_parts, share(q % n_y, rows // n_y), near_col, slab, n_y)
    amp_near = exchanged(near_slab, y_groups).reshape(rows, rows)
    near_density = first_density(amp_near, [near], tile)

    first_products = products(own, [far[0], after(far[1], near_density)], depth_tile)
    last_products = products(own, [after(far[2], first_products)], depth_tile)
    far_products = jnp.concatenate([first_products, last_products], axis=1)
    far_parts = lax.all_to_all(far_products.reshape(n_aux, rows // n_aux, rows), "aux", 0, 0)
    far_slab = amplitudes(far_parts, share(q, rows // n_aux), far_col, slab, n_aux)
    amp_far = lax.all_to_all(far_slab, "aux", 0, 0).reshape(rows, rows)
    gamma = last_density(amp_far, far, near_density, tile)
    return gamma.reshape(occ_rows, slab, cols)


def solution(mesh):
    placed = (P("occ", None, "aux"), P("occ"), P())
    return jax.shard_map(
        per_device, mesh=mesh, in_specs=placed, out_specs=P("occ", None, "aux"), check_vma=False
    )
```
